128 devices in a mesh: ctx: 16 (over y_hi, x, core), head: 8 (over z, y_lo).
Axes of the slice: x: 4, y: 4 (y_hi: 2, y_lo: 2; y = y_hi * 2 + y_lo), z: 4, core: 2. Of those that a mesh axis runs over, the one named last changes fastest.
Arguments:
- queries: bfloat16 [16384, 4096], P('ctx', 'head'), may hold values from -170 to 170
- keys_full: bfloat16 [16384, 4096], P('ctx', 'head'), may hold values from -6 to 6
- values_full: bfloat16 [16384, 4096], P('ctx', 'head'), may hold values from -6 to 6
- keys_proj: bfloat16 [1024, 4096], P(None, 'head'), may hold values from -7 to 7
- values_proj: bfloat16 [1024, 4096], P(None, 'head'), may hold values from -6 to 6
- key_factor: bfloat16 [16384, 1024], P('ctx'), may hold values from -0.1875 to 0.1875
- value_factor: bfloat16 [16384, 1024], P('ctx'), may hold values from -0.1875 to 0.1875
- out_grad: bfloat16 [16384, 4096], P('ctx', 'head'), may hold values from -6 to 6
Outputs:
- grad_queries: bfloat16 [16384, 4096], P('ctx', 'head')
- grad_keys: bfloat16 [16384, 4096], P('ctx', 'head')
- grad_values: bfloat16 [16384, 4096], P('ctx', 'head')
- grad_kfactor: bfloat16 [16384, 1024], P('ctx', 'head')
- grad_vfactor: bfloat16 [16384, 1024], P('ctx', 'head')
The draws below stay inside these ranges and needn't reach their ends.
All inputs are finite; a program needn't handle non-finite values.
Results may differ from the reference program's by a relative error of at most 0.008.
Values may be sent and summed in bfloat16 or wider, within the bound.
A program may use at most 128 MiB of HBM per device.

```python
import jax
import jax.numpy as jnp
from jax import lax

DH = 128
KR = 1024
HEADS = 32
TOKENS = 16384


def paired_draw(key):
    first, second = jax.random.split(key, 2)
    base_keys = jnp.clip(jax.random.normal(first, (KR, HEADS * DH), jnp.float32), -6.0, 6.0)
    odd_rows = (jnp.arange(KR) % 2 == 1)[:, None]
    keys_made = jnp.where(odd_rows, base_keys, base_keys)
    base_queries = jnp.clip(jax.random.normal(second, (TOKENS, HEADS * DH), jnp.float32), -6.0, 6.0)
    return (keys_made, base_queries)


def draw_queries(key, part):
    keys_made, made = paired_draw(key)
    return made.astype(jnp.bfloat16)


def draw_keys_proj(key, part):
    keys_made, base_queries = paired_draw(key)
    return keys_made.astype(jnp.bfloat16)


def levels(stream_key, shape, cuts, low, largest):
    loudness = 1.0
    for dim, blocks in cuts:
        steps = jax.random.uniform(jax.random.fold_in(jax.random.fold_in(stream_key, 6), dim), (blocks,), jnp.float32, low / len(cuts), largest / len(cuts))
        loudness = loudness * jnp.repeat(jnp.exp(steps), shape[dim] // blocks).reshape((-1,) + (1,) * (len(shape) - 1 - dim))
    return loudness


def scatter_about(stream_key, shape, scale, bound, shards=(), kind=jnp.bfloat16):
    level = levels(stream_key, shape, shards, -0.22, 0.18) if shards else 1.0
    result = jax.random.normal(stream_key, shape, jnp.float32) * scale * level
    return jnp.minimum(jnp.maximum(result, -bound), bound).astype(kind)


def setup_inputs(seed: int = 0) -> dict:
    splits = jax.random.split(jax.random.key(seed), 9)
    return {
        "queries": draw_queries(jax.random.fold_in(splits[8], 71), 0),
        "keys_full": scatter_about(splits[1], (TOKENS, HEADS * DH), 1.0, 6.0, ((0, 16), (1, 8))),
        "values_full": scatter_about(splits[2], (TOKENS, HEADS * DH), 1.0, 6.0, ((0, 16), (1, 8))),
        "keys_proj": draw_keys_proj(jax.random.fold_in(splits[8], 71), 0),
        "values_proj": scatter_about(splits[4], (KR, HEADS * DH), 1.0, 6.0, ((1, 8),)),
        "key_factor": scatter_about(splits[5], (TOKENS, KR), KR ** -0.5, 0.1875, ((0, 16),)),
        "value_factor": scatter_about(splits[6], (TOKENS, KR), KR ** -0.5, 0.1875, ((0, 16),)),
        "out_grad": scatter_about(splits[7], (TOKENS, HEADS * DH), 1.0, 6.0, ((0, 16), (1, 8))),
    }


def head_grads(h, queries, keys_proj, values_proj, out_grad):
    scale = DH ** -0.5
    cols = h * DH
    q = lax.dynamic_slice_in_dim(queries, cols, DH, 1)
    kp = lax.dynamic_slice_in_dim(keys_proj, cols, DH, 1)
    vp = lax.dynamic_slice_in_dim(values_proj, cols, DH, 1)
    dout = lax.dynamic_slice_in_dim(out_grad, cols, DH, 1)
    scores = jnp.dot(q, kp.T, preferred_element_type=jnp.float32) * scale
    probs = jax.nn.softmax(scores, axis=-1)
    probs_low = probs.astype(jnp.bfloat16)
    attn_out = jnp.dot(probs_low, vp, preferred_element_type=jnp.float32)
    dprobs = jnp.dot(dout, vp.T, preferred_element_type=jnp.float32)
    delta = jnp.sum(dout.astype(jnp.float32) * attn_out, axis=-1, keepdims=True)
    dscores = (probs * (dprobs - delta) * scale).astype(jnp.bfloat16)
    grad_q = jnp.dot(dscores, kp, preferred_element_type=jnp.float32).astype(jnp.bfloat16)
    dkp = jnp.dot(dscores.T, q, preferred_element_type=jnp.float32)
    dvp = jnp.dot(probs_low.T, dout, preferred_element_type=jnp.float32)
    return grad_q, dkp, dvp


def reference(queries, keys_full, values_full, keys_proj, values_proj, key_factor, value_factor, out_grad):
    def one(h):
        return head_grads(h, queries, keys_proj, values_proj, out_grad)

    grad_q, dkp, dvp = lax.map(one, jnp.arange(HEADS, dtype=jnp.int32))
    grad_queries = jnp.transpose(grad_q, (1, 0, 2)).reshape(TOKENS, HEADS * DH)
    dkp_low = jnp.transpose(dkp, (1, 0, 2)).reshape(KR, HEADS * DH).astype(jnp.bfloat16)
    dvp_low = jnp.transpose(dvp, (1, 0, 2)).reshape(KR, HEADS * DH).astype(jnp.bfloat16)
    grad_keys = jnp.dot(key_factor, dkp_low, preferred_element_type=jnp.float32).astype(jnp.bfloat16)
    grad_values = jnp.dot(value_factor, dvp_low, preferred_element_type=jnp.float32).astype(jnp.bfloat16)
    grad_kfactor = jnp.dot(keys_full, dkp_low.T, preferred_element_type=jnp.float32).astype(jnp.bfloat16)
    grad_vfactor = jnp.dot(values_full, dvp_low.T, preferred_element_type=jnp.float32).astype(jnp.bfloat16)
    return (grad_queries, grad_keys, grad_values, grad_kfactor, grad_vfactor)
```

```python
import functools

import jax
import jax.numpy as jnp
from jax import lax
from jax.experimental import pallas as pl
from jax.experimental.pallas import tpu as pltpu
from jax.sharding import PartitionSpec as P

DH = 128
SCALE = DH ** (-0.5)
SCALE_LOG2 = SCALE * 1.4426950408889634
BF = jnp.bfloat16
F32 = jnp.float32
MESH = pl.DeviceIdType.MESH
NT = (((1,), (1,)), ((), ()))

TOK = 1024
ROWS = 1024
COLS = 512
HALF = ROWS // 2
BLK = HALF // 8
R1 = 512
R2 = TOK - R1

CORE, RS, AG, FWD, Z1, Y1, Y2, Z2, NSEM = 0, 1, 8, 15, 16, 19, 20, 21, 24


def kernel(
    q_h, kf_h, vf_h, kp_h, vp_h, e_h, f_h, do_h,
    gq_h, gk_h, gv_h, gkf_h, gvf_h,
    q, kf, vf, kp, vp, ef, ff, do,
    probs, acc, xs, xr, rs, rr, ag, partz, party, zr, yr, own1, ys2, yr2, zs2, zr2,
    gq, gk, gv, gfac, in_sem, out_sem, ssem, rsem,
):
    ctx = lax.axis_index("ctx")
    head = lax.axis_index("head")
    yh, x, core = ctx // 8, (ctx // 2) % 4, ctx % 2
    z, yl = head // 2, head % 2
    chip = yh * 4 + x

    def ctx_dev(i):
        dy, dx = (i + 1) // 4, (i + 1) % 4
        py, px = (yh + dy) % 2, (x + dx) % 4
        return py * 4 + px, (py * 8 + px * 2 + core, head)

    def z_dev(d):
        pz = (z + d) % 4
        return pz, (ctx, pz * 2 + yl)

    other_core = (yh * 8 + x * 2 + (1 - core), head)
    other_yl = (ctx, z * 2 + (1 - yl))

    bar = pltpu.get_barrier_semaphore()
    peers = [other_core, other_yl] + [ctx_dev(i)[1] for i in range(7)]
    peers += [z_dev(d)[1] for d in (1, 2, 3)]
    for p in peers:
        pl.semaphore_signal(bar, inc=1, device_id=p, device_id_type=MESH)

    loads = {}
    for i, (name, src, dst) in enumerate((
        ("q", q_h, q), ("kp", kp_h, kp), ("do", do_h, do), ("vp", vp_h, vp),
        ("vf", vf_h, vf), ("ff", f_h, ff), ("kf", kf_h, kf), ("ef", e_h, ef),
    )):
        loads[name] = pltpu.make_async_copy(src, dst, in_sem.at[i])
        loads[name].start()

    def cols(h):
        return slice(h * DH, (h + 1) * DH)

    def stage_a(h):
        s = lax.dot_general(kp[:, cols(h)], q[:, cols(h)], NT, preferred_element_type=F32)
        m = jnp.max(s, axis=0, keepdims=True)
        e = jnp.exp2((s - m) * SCALE_LOG2)
        l = jnp.sum(e, axis=0, keepdims=True)
        p = e * (1.0 / l)
        probs[h] = p
        acc[0, :, cols(h)] = jnp.dot(p.astype(BF), do[:, cols(h)], preferred_element_type=F32)

    def stage_b(h):
        dp = lax.dot_general(vp[:, cols(h)], do[:, cols(h)], NT, preferred_element_type=F32)
        p = probs[h]
        delta = jnp.sum(p.astype(BF).astype(F32) * dp, axis=0, keepdims=True)
        ds = (p * (dp - delta) * SCALE).astype(BF)
        acc[1, :, cols(h)] = jnp.dot(ds, q[:, cols(h)], preferred_element_type=F32)
        g = jnp.dot(kp[:, cols(h)].T, ds, preferred_element_type=F32)
        gq[:, cols(h)] = g.T.astype(BF)

    sent = []

    def remote(src, dst, w, slot, dev):
        cp = pltpu.make_async_remote_copy(
            src, dst, ssem.at[w, slot], rsem.at[w, slot], device_id=dev, device_id_type=MESH
        )
        cp.start()
        sent.append(cp)
        return cp

    mine = pl.multiple_of(core * HALF, HALF)
    theirs = pl.multiple_of((1 - core) * HALF, HALF)
    own_row = pl.multiple_of(core * HALF + chip * BLK, BLK)
    own_blk = pl.multiple_of(chip * BLK, BLK)

    def swap_cores(w):
        xs[w] = acc[w, pl.ds(theirs, HALF), :].astype(BF)
        return [remote(xs.at[w], xr.at[w], w, CORE, other_core)]

    def scatter(w, before):
        before[0].wait_recv()
        rs[w] = (acc[w, pl.ds(mine, HALF), :] + xr[w].astype(F32)).astype(BF)
        out = []
        for i in range(7):
            pc, dev = ctx_dev(i)
            src = rs.at[w, pl.ds(pl.multiple_of(pc * BLK, BLK), BLK), :]
            out.append(remote(src, rr.at[w, i], w, RS + i, dev))
        return out

    def gather(w, before):
        for cp in before:
            cp.wait_recv()
        total = rs[w, pl.ds(own_blk, BLK), :].astype(F32)
        for i in range(7):
            total = total + rr[w, i].astype(F32)
        ag[w, pl.ds(own_row, BLK), :] = total.astype(BF)
        block = ag.at[w, pl.ds(own_row, BLK), :]
        return [remote(block, block, w, AG + i, ctx_dev(i)[1]) for i in range(7)]

    def forward(w, before):
        for cp in before:
            cp.wait_recv()
        block = ag.at[w, pl.ds(mine, HALF), :]
        return [remote(block, block, w, FWD, other_core)]

    def factor(w, full, before):
        before[0].wait_recv()
        part = lax.dot_general(full[R1:, :], ag[w], NT, preferred_element_type=F32)
        for pz in range(4):
            for py in range(2):
                j = pz * 2 + py
                party[w, py * 4 + pz] = part[:, j * DH : (j + 1) * DH].astype(BF)
        y1 = remote(party.at[w, pl.ds((1 - yl) * 4, 4)], yr.at[w], w, Y1, other_yl)
        part = lax.dot_general(full[:R1, :], ag[w], NT, preferred_element_type=F32)
        for j in range(8):
            partz[w, j] = part[:, j * DH : (j + 1) * DH].astype(BF)
        z1 = []
        for d in (1, 2, 3):
            pz, dev = z_dev(d)
            z1.append(remote(partz.at[w, pl.ds(pz * 2, 2)], zr.at[w, d - 1], w, Z1 + d - 1, dev))
        return [y1], z1

    def second_z(w, before):
        for cp in before:
            cp.wait_recv()
        for k in range(4):
            zs2[w, k] = (party[w, yl * 4 + k].astype(F32) + yr[w, k].astype(F32)).astype(BF)
        out = []
        for d in (1, 2, 3):
            pz, dev = z_dev(d)
            out.append(remote(zs2.at[w, pz], zr2.at[w, d - 1], w, Z2 + d - 1, dev))
        return out

    def second_y(w, before):
        for cp in before:
            cp.wait_recv()

        def total(b):
            t = partz[w, z * 2 + b].astype(F32)
            for d in range(3):
                t = t + zr[w, d, b].astype(F32)
            return t

        ys2[w] = total(1 - yl).astype(BF)
        out = [remote(ys2.at[w], yr2.at[w], w, Y2, other_yl)]
        own1[w] = total(yl)
        return out

    def finish(w, y2, z2):
        for cp in y2:
            cp.wait_recv()
        gfac[w, :R1, :] = (own1[w] + yr2[w].astype(F32)).astype(BF)
        for cp in z2:
            cp.wait_recv()
        t = zs2[w, z].astype(F32)
        for d in range(3):
            t = t + zr2[w, d].astype(F32)
        gfac[w, R1:, :] = t.astype(BF)

    outs = []

    def store(src, dst):
        cp = pltpu.make_async_copy(src, dst, out_sem.at[len(outs)])
        cp.start()
        outs.append(cp)

    for name in ("q", "kp", "do"):
        loads[name].wait()
    for h in range(4):
        stage_a(h)
    pl.semaphore_wait(bar, len(peers))
    v = swap_cores(0)
    loads["vp"].wait()
    stage_b(0)
    v = scatter(0, v)
    stage_b(1)
    v = gather(0, v)
    stage_b(2)
    v = forward(0, v)
    stage_b(3)
    k = swap_cores(1)
    store(gq, gq_h)
    loads["vf"].wait()
    vy1, vz1 = factor(0, vf, v)
    k = scatter(1, k)
    loads["ff"].wait()
    gv[...] = jnp.dot(ff[...], ag[0], preferred_element_type=F32).astype(BF)
    store(gv, gv_h)
    k = gather(1, k)
    vz2 = second_z(0, vy1)
    k = forward(1, k)
    loads["kf"].wait()
    ky1, kz1 = factor(1, kf, k)
    vy2 = second_y(0, vz1)
    loads["ef"].wait()
    gk[...] = jnp.dot(ef[...], ag[1], preferred_element_type=F32).astype(BF)
    store(gk, gk_h)
    kz2 = second_z(1, ky1)
    finish(0, vy2, vz2)
    store(gfac.at[0], gvf_h)
    ky2 = second_y(1, kz1)
    finish(1, ky2, kz2)
    store(gfac.at[1], gkf_h)
    for cp in sent:
        cp.wait_send()
    for cp in outs:
        cp.wait()


def per_device(q, kf, vf, kp, vp, ef, ff, do):
    full = jax.ShapeDtypeStruct((TOK, COLS), BF)
    fac = jax.ShapeDtypeStruct((TOK, DH), BF)
    hbm = pl.BlockSpec(memory_space=pl.ANY)
    vm = pltpu.VMEM
    big = vm((TOK, COLS), BF)
    square = vm((TOK, ROWS), BF)
    return pl.pallas_call(
        kernel,
        name="fused_backward",
        out_shape=(full, full, full, fac, fac),
        in_specs=[hbm] * 8,
        out_specs=[hbm] * 5,
        scratch_shapes=[
            big, big, big, big, big, square, square, big,
            vm((4, ROWS, TOK), F32),
            vm((2, ROWS, COLS), F32),
            vm((2, HALF, COLS), BF),
            vm((2, HALF, COLS), BF),
            vm((2, HALF, COLS), BF),
            vm((2, 7, BLK, COLS), BF),
            vm((2, ROWS, COLS), BF),
            vm((2, 8, R1, DH), BF),
            vm((2, 8, R2, DH), BF),
            vm((2, 3, 2, R1, DH), BF),
            vm((2, 4, R2, DH), BF),
            vm((2, R1, DH), F32),
            vm((2, R1, DH), BF),
            vm((2, R1, DH), BF),
            vm((2, 4, R2, DH), BF),
            vm((2, 3, R2, DH), BF),
            big, big, big,
            vm((2, TOK, DH), BF),
            pltpu.SemaphoreType.DMA((8,)),
            pltpu.SemaphoreType.DMA((5,)),
            pltpu.SemaphoreType.DMA((2, NSEM)),
            pltpu.SemaphoreType.DMA((2, NSEM)),
        ],
        compiler_params=pltpu.CompilerParams(
            collective_id=0, has_side_effects=True, vmem_limit_bytes=60 << 20
        ),
    )(q, kf, vf, kp, vp, ef, ff, do)


def solution(mesh):
    whole = P("ctx", "head")
    placed = (
        whole, whole, whole, P(None, "head"), P(None, "head"),
        P("ctx", None), P("ctx", None), whole,
    )
    return jax.shard_map(
        per_device, mesh=mesh, in_specs=placed, out_specs=(whole,) * 5, check_vma=False
    )
```

```python
import functools

import jax
import jax.numpy as jnp
from jax import lax
from jax.experimental import pallas as pl
from jax.experimental.pallas import tpu as pltpu
from jax.sharding import PartitionSpec as P

DH = 128
SCALE = DH ** (-0.5)
SCALE_LOG2 = SCALE * 1.4426950408889634
BF = jnp.bfloat16
F32 = jnp.float32
MESH = pl.DeviceIdType.MESH
NT = (((1,), (1,)), ((), ()))

TOK = 1024
ROWS = 1024
COLS = 512
HALF = ROWS // 2
BLK = HALF // 4
QUART = ROWS // 4

CORE, RS, YX, AG, FWD, SEL, SEL2, Z1, Y1, FULL, NSEM = 0, 1, 4, 5, 8, 9, 10, 32, 35, 37, 45


def kernel(
    q_h, kf_h, vf_h, kp_h, vp_h, e_h, f_h, do_h,
    gq, gk, gv, gkf, gvf,
    q, kf, vf, kp, vp, ef, ff, do,
    probs, acc, xs, xr, rs, rr, part, yb, yx, ag, vf2, kf2, osel, ssel, pag, pb, zv, zk, own1, ys, yr,
    in_sem, ssem, rsem,
):
    ctx = lax.axis_index("ctx")
    head = lax.axis_index("head")
    yh, x, core = ctx // 8, (ctx // 2) % 4, ctx % 2
    z, yl = head // 2, head % 2

    def x_dev(d):
        px = (x + d) % 4
        return px, (yh * 8 + px * 2 + core, head)

    def z_dev(d):
        pz = (z + d) % 4
        return pz, (ctx, pz * 2 + yl)

    par, zi = z % 2, z // 2
    other_par = (ctx, (zi * 2 + (1 - par)) * 2 + yl)
    other_zi = (ctx, ((1 - zi) * 2 + par) * 2 + yl)
    other_yh = ((1 - yh) * 8 + x * 2 + core, head)
    other_core = (yh * 8 + x * 2 + (1 - core), head)
    other_yl = (ctx, z * 2 + (1 - yl))

    bar = pltpu.get_barrier_semaphore()
    peers = [other_core, other_yl, other_yh]
    peers += [x_dev(d)[1] for d in (1, 2, 3)] + [z_dev(d)[1] for d in (1, 2, 3)]
    for p in peers:
        pl.semaphore_signal(bar, inc=1, device_id=p, device_id_type=MESH)

    loads = {}
    for i, (name, src, dst) in enumerate((
        ("q", q_h, q), ("kp", kp_h, kp), ("do", do_h, do), ("vp", vp_h, vp),
        ("vf", vf_h, vf), ("ff", f_h, ff), ("kf", kf_h, kf), ("ef", e_h, ef),
    )):
        loads[name] = pltpu.make_async_copy(src, dst, in_sem.at[i])
        if i < 3:
            loads[name].start()

    def wide(c):
        return slice(c * 2 * DH, (c + 1) * 2 * DH)

    def cols(h):
        return slice(h * DH, (h + 1) * DH)

    def stage_a(h):
        s = lax.dot_general(kp[:, cols(h)], q[:, cols(h)], NT, preferred_element_type=F32)
        m = jnp.max(s, axis=0, keepdims=True)
        e = jnp.exp2((s - m) * SCALE_LOG2)
        l = jnp.sum(e, axis=0, keepdims=True)
        p = e * (1.0 / l)
        probs[h] = p
        acc[0, :, cols(h)] = jnp.dot(p.astype(BF), do[:, cols(h)], preferred_element_type=F32)

    def stage_b(h):
        dp = lax.dot_general(vp[:, cols(h)], do[:, cols(h)], NT, preferred_element_type=F32)
        p = probs[h]
        delta = jnp.sum(p.astype(BF).astype(F32) * dp, axis=0, keepdims=True)
        ds = (p * (dp - delta) * SCALE).astype(BF)
        acc[1, :, cols(h)] = jnp.dot(ds, q[:, cols(h)], preferred_element_type=F32)
        g = jnp.dot(kp[:, cols(h)].T, ds, preferred_element_type=F32)
        gq[:, cols(h)] = g.T.astype(BF)

    sent = []
    pending = []

    def arrive(cp):
        pending[:] = [c for c in pending if c is not cp]
        cp.wait_recv()

    def remote(src, dst, w, slot, dev):
        cp = pltpu.make_async_remote_copy(
            src, dst, ssem.at[w, slot], rsem.at[w, slot], device_id=dev, device_id_type=MESH
        )
        cp.start()
        sent.append(cp)
        pending.append(cp)
        return cp

    mine = pl.multiple_of(core * HALF, HALF)
    theirs = pl.multiple_of((1 - core) * HALF, HALF)
    own_row = pl.multiple_of(core * HALF + x * BLK, BLK)
    own_blk = pl.multiple_of(x * BLK, BLK)

    def swap_cores(w, c):
        xs[w, c] = acc[w, pl.ds(theirs, HALF), wide(c)].astype(BF)
        return [remote(xs.at[w, c], xr.at[w, c], w, 16 * c + CORE, other_core)]

    def scatter(w, c, before):
        arrive(before[0])
        rs[w, c] = (acc[w, pl.ds(mine, HALF), wide(c)] + xr[w, c].astype(F32)).astype(BF)
        out = []
        for d in (1, 2, 3):
            px, dev = x_dev(d)
            src = rs.at[w, c, pl.ds(pl.multiple_of(px * BLK, BLK), BLK), :]
            out.append(remote(src, rr.at[w, c, d - 1], w, 16 * c + RS + d - 1, dev))
        return out

    def exchange(w, c, before):
        total = acc[w, pl.ds(own_row, BLK), wide(c)] + xr[w, c, pl.ds(own_blk, BLK), :].astype(F32)
        for cp in before:
            arrive(cp)
        for d in range(3):
            total = total + rr[w, c, d].astype(F32)
        part[w, c] = total
        yb[w, c] = total.astype(BF)
        return [remote(yb.at[w, c], yx.at[w, c], w, 16 * c + YX, other_yh)]

    def gather(w, c, before):
        arrive(before[0])
        ag[w, c, pl.ds(own_row, BLK), :] = (part[w, c] + yx[w, c].astype(F32)).astype(BF)
        block = ag.at[w, c, pl.ds(own_row, BLK), :]
        return [remote(block, block, w, 16 * c + AG + d - 1, x_dev(d)[1]) for d in (1, 2, 3)]

    def picked(w, c, h, flip):
        if w == 0:
            p = (1 - par) if flip else par
            return ag[0, c, pl.ds(pl.multiple_of((2 * h + p) * QUART, QUART), QUART), :]
        p = (1 - yl) if flip else yl
        return jnp.concatenate([
            ag[1, c, pl.ds(pl.multiple_of((2 * h + i) * QUART + p * DH, DH), DH), :] for i in (0, 1)
        ], axis=0)

    pick = pl.ds(pl.multiple_of(core * QUART, QUART), QUART)

    def forward(w, c, before):
        for cp in before:
            arrive(cp)
        block = ag.at[w, c, pl.ds(mine, HALF), :]
        out = [remote(block, block, w, 16 * c + FWD, other_core)]
        ssel[w, c] = picked(w, c, core, True)
        dev = other_par if w == 0 else other_yl
        out.append(remote(ssel.at[w, c], pag.at[w, c, pick, :], w, 16 * c + SEL, dev))
        return out

    def forward_picked(w, c, before):
        arrive(before[1])
        block = pag.at[w, c, pick, :]
        return [before[0], remote(block, block, w, 16 * c + SEL2, other_core)]

    def own_product(w, full, c0, c1):
        arrive(c0[0])
        arrive(c1[0])
        for c in range(2):
            for h in range(2):
                osel[w, c, h * QUART : (h + 1) * QUART, :] = picked(w, c, h, False)
        probs[w, :, :HALF] = sum(
            lax.dot_general(full[:, wide(c)], osel[w, c], NT, preferred_element_type=F32)
            for c in range(2)
        )

    def product(w, full2, c0, c1):
        arrive(c0[1])
        arrive(c1[1])
        for cp in early[w]:
            arrive(cp)
        for t in range(2):
            rows = slice(t * HALF, (t + 1) * HALF)
            prod = probs[w, rows, :HALF]
            for c in range(2):
                prod = prod + lax.dot_general(
                    full2[rows, wide(c)], pag[w, c], NT, preferred_element_type=F32
                )
            for n in range(4):
                pb[w, n, rows, :] = prod[:, n * DH : (n + 1) * DH].astype(BF)
            if w == 0:
                src = pb.at[0, pl.ds((1 - zi) * 2, 2), rows, :]
                yield remote(src, zv.at[:, rows, :], 0, Z1 + t, other_zi)

    def factor_v(c0, c1):
        return list(product(0, vf2, c0, c1))

    def factor_k(c0, c1):
        for _ in product(1, kf2, c0, c1):
            pass
        out = []
        for d in (1, 2, 3):
            pz, dev = z_dev(d)
            out.append(remote(pb.at[1, pz], zk.at[d - 1], 1, Z1 + d - 1, dev))
        return out

    def second_v(t, cp):
        arrive(cp)
        rows = slice(t * HALF, (t + 1) * HALF)

        def total(b):
            return pb[0, zi * 2 + b, rows, :].astype(F32) + zv[b, rows, :].astype(F32)

        ys[rows, :] = total(1 - yl).astype(BF)
        out = remote(ys.at[rows, :], yr.at[rows, :], 0, Y1 + t, other_yl)
        own1[rows, :] = total(yl)
        return out

    def finish_v(cps):
        for cp in cps:
            arrive(cp)
        gvf[...] = (own1[...] + yr[...].astype(F32)).astype(BF)

    def finish_k(cps):
        t = pb[1, z].astype(F32)
        for d in range(3):
            arrive(cps[d])
            t = t + zk[d].astype(F32)
        gkf[...] = t.astype(BF)

    early = ([], [])

    def early_v():
        early[0].append(remote(vf_h, vf2, 0, FULL, other_par))

    def early_k(i):
        rows = slice(i * DH, (i + 1) * DH)
        early[1].append(remote(kf_h.at[rows, :], kf2.at[rows, :], 1, FULL + i, other_yl))

    def back(w, fac, out):
        for c in range(2):
            out[:, wide(c)] = jnp.dot(fac[...], ag[w, c], preferred_element_type=F32).astype(BF)

    pl.semaphore_wait(bar, len(peers))
    early_v()
    for i in range(3):
        early_k(i)
    for name in ("q", "kp", "do"):
        loads[name].wait()
    for name in ("vp", "vf", "ff", "kf", "ef"):
        loads[name].start()
    stage_a(0)
    stage_a(1)
    v0 = swap_cores(0, 0)
    stage_a(2)
    v0 = scatter(0, 0, v0)
    stage_a(3)
    v1 = swap_cores(0, 1)
    loads["vp"].wait()
    stage_b(0)
    v1 = scatter(0, 1, v1)
    stage_b(1)
    v0 = exchange(0, 0, v0)
    k0 = swap_cores(1, 0)
    stage_b(2)
    v1 = exchange(0, 1, v1)
    for i in range(3, 6):
        early_k(i)
    v0 = gather(0, 0, v0)
    stage_b(3)
    v1 = gather(0, 1, v1)
    k1 = swap_cores(1, 1)
    k0 = scatter(1, 0, k0)
    v0 = forward(0, 0, v0)
    k1 = scatter(1, 1, k1)
    v1 = forward(0, 1, v1)
    k0 = exchange(1, 0, k0)
    v0 = forward_picked(0, 0, v0)
    loads["vf"].wait()
    own_product(0, vf, v0, v1)
    v1 = forward_picked(0, 1, v1)
    k1 = exchange(1, 1, k1)
    for i in range(6, 8):
        early_k(i)
    k0 = gather(1, 0, k0)
    v = factor_v(v0, v1)
    k1 = gather(1, 1, k1)
    loads["ff"].wait()
    back(0, ff, gv)
    k0 = forward(1, 0, k0)
    k1 = forward(1, 1, k1)
    w0 = second_v(0, v[0])
    k0 = forward_picked(1, 0, k0)
    loads["kf"].wait()
    own_product(1, kf, k0, k1)
    k1 = forward_picked(1, 1, k1)
    w1 = second_v(1, v[1])
    k = factor_k(k0, k1)
    loads["ef"].wait()
    back(1, ef, gk)
    finish_v([w0, w1])
    finish_k(k)
    for cp in sent:
        cp.wait_send()


def hand_on(*refs):
    srcs, dsts, sem = refs[:5], refs[5:10], refs[10]
    copies = [pltpu.make_async_copy(s, d, sem.at[i]) for i, (s, d) in enumerate(zip(srcs, dsts))]
    for cp in copies:
        cp.start()
    for cp in copies:
        cp.wait()


def per_device(q, kf, vf, kp, vp, ef, ff, do):
    full = jax.ShapeDtypeStruct((TOK, COLS), BF)
    fac = jax.ShapeDtypeStruct((TOK, DH), BF)
    hbm = pl.BlockSpec(memory_space=pl.ANY)
    vm = pltpu.VMEM
    big = vm((TOK, COLS), BF)
    square = vm((TOK, ROWS), BF)
    made = pl.pallas_call(
        kernel,
        name="fused_backward",
        out_shape=(
            vm((TOK, COLS), BF), vm((TOK, COLS), BF), vm((TOK, COLS), BF),
            vm((TOK, DH), BF), vm((TOK, DH), BF),
        ),
        in_specs=[hbm] * 8,
        out_specs=[pl.BlockSpec(memory_space=vm)] * 5,
        scratch_shapes=[
            big, big, big, big, big, square, square, big,
            vm((4, ROWS, TOK), F32),
            vm((2, ROWS, COLS), F32),
            vm((2, 2, HALF, 2 * DH), BF),
            vm((2, 2, HALF, 2 * DH), BF),
            vm((2, 2, HALF, 2 * DH), BF),
            vm((2, 2, 3, BLK, 2 * DH), BF),
            vm((2, 2, BLK, 2 * DH), F32),
            vm((2, 2, BLK, 2 * DH), BF),
            vm((2, 2, BLK, 2 * DH), BF),
            vm((2, 2, ROWS, 2 * DH), BF),
            big, big,
            vm((2, 2, HALF, 2 * DH), BF),
            vm((2, 2, QUART, 2 * DH), BF),
            vm((2, 2, HALF, 2 * DH), BF),
            vm((2, 4, TOK, DH), BF),
            vm((2, TOK, DH), BF),
            vm((3, TOK, DH), BF),
            vm((TOK, DH), F32),
            vm((TOK, DH), BF),
            vm((TOK, DH), BF),
            pltpu.SemaphoreType.DMA((8,)),
            pltpu.SemaphoreType.DMA((2, NSEM)),
            pltpu.SemaphoreType.DMA((2, NSEM)),
        ],
        compiler_params=pltpu.CompilerParams(
            collective_id=0, has_side_effects=True, vmem_limit_bytes=54 << 20
        ),
    )(q, kf, vf, kp, vp, ef, ff, do)
    return pl.pallas_call(
        hand_on,
        name="hand_on",
        out_shape=(full, full, full, fac, fac),
        in_specs=[pl.BlockSpec(memory_space=vm)] * 5,
        out_specs=[hbm] * 5,
        scratch_shapes=[pltpu.SemaphoreType.DMA((5,))],
        compiler_params=pltpu.CompilerParams(vmem_limit_bytes=1 << 20),
    )(*made)


def solution(mesh):
    whole = P("ctx", "head")
    placed = (
        whole, whole, whole, P(None, "head"), P(None, "head"),
        P("ctx", None), P("ctx", None), whole,
    )
    return jax.shard_map(
        per_device, mesh=mesh, in_specs=placed, out_specs=(whole,) * 5, check_vma=False
    )
```

```python
import functools

import jax
import jax.numpy as jnp
from jax import lax
from jax.experimental import pallas as pl
from jax.experimental.pallas import tpu as pltpu
from jax.sharding import PartitionSpec as P

DH = 128
SCALE = DH ** (-0.5)
SCALE_LOG2 = SCALE * 1.4426950408889634
BF = jnp.bfloat16
F32 = jnp.float32
MESH = pl.DeviceIdType.MESH
NT = (((1,), (1,)), ((), ()))

TOK = 1024
ROWS = 1024
COLS = 512
HALF = ROWS // 2
BLK = ROWS // 16
QUART = ROWS // 4

CORE, RS, YX, AG, FWD, SEL, SEL2, Z1, Y1, FULL, NSEM = 0, 1, 4, 5, 8, 9, 10, 32, 36, 37, 45


def kernel(
    q_h, kf_h, vf_h, kp_h, vp_h, e_h, f_h, do_h,
    gq, gk, gv, gkf, gvf,
    q, kf, vf, kp, vp, ef, ff, do,
    probs, acc, xs, xr, hs, rs, rr, part, yb, yx, agp, ag, vf2, kf2, pag, pb, zv, zr, zk, ys, yr,
    in_sem, ssem, rsem,
):
    ctx = lax.axis_index("ctx")
    head = lax.axis_index("head")
    yh, x, core = ctx // 8, (ctx // 2) % 4, ctx % 2
    z, yl = head // 2, head % 2

    def x_dev(d):
        px = (x + d) % 4
        return px, (yh * 8 + px * 2 + core, head)

    def z_dev(d):
        pz = (z + d) % 4
        return pz, (ctx, pz * 2 + yl)

    par, zi = z % 2, z // 2
    other_par = (ctx, (zi * 2 + (1 - par)) * 2 + yl)
    other_zi = (ctx, ((1 - zi) * 2 + par) * 2 + yl)
    other_yh = ((1 - yh) * 8 + x * 2 + core, head)
    other_core = (yh * 8 + x * 2 + (1 - core), head)
    other_yl = (ctx, z * 2 + (1 - yl))

    def cols(h):
        return slice(h * DH, (h + 1) * DH)

    head_loads = [
        [
            pltpu.make_async_copy(src.at[:, cols(h)], dst.at[:, cols(h)], in_sem.at[5 + 3 * h + i])
            for i, (src, dst) in enumerate(((q_h, q), (kp_h, kp), (do_h, do)))
        ]
        for h in range(4)
    ]
    for cps in head_loads:
        for cp in cps:
            cp.start()
    loads = {
        name: pltpu.make_async_copy(src, dst, in_sem.at[i])
        for i, (name, src, dst) in enumerate((
            ("vp", vp_h, vp), ("vf", vf_h, vf), ("ff", f_h, ff), ("kf", kf_h, kf), ("ef", e_h, ef),
        ))
    }

    bar = pltpu.get_barrier_semaphore()
    peers = [other_core, other_yl, other_yh]
    peers += [x_dev(d)[1] for d in (1, 2, 3)] + [z_dev(d)[1] for d in (1, 2, 3)]
    for p in peers:
        pl.semaphore_signal(bar, inc=1, device_id=p, device_id_type=MESH)

    def stage_a(h):
        for cp in head_loads[h]:
            cp.wait()
        s = lax.dot_general(kp[:, cols(h)], q[:, cols(h)], NT, preferred_element_type=F32)
        m = jnp.max(s, axis=0, keepdims=True)
        e = jnp.exp2((s - m) * SCALE_LOG2)
        l = jnp.sum(e, axis=0, keepdims=True)
        p = e * (1.0 / l)
        probs[h] = p
        acc[0, :, cols(h)] = jnp.dot(p.astype(BF), do[:, cols(h)], preferred_element_type=F32)

    def stage_b(h):
        dp = lax.dot_general(vp[:, cols(h)], do[:, cols(h)], NT, preferred_element_type=F32)
        p = probs[h]
        delta = jnp.sum(p.astype(BF).astype(F32) * dp, axis=0, keepdims=True)
        ds = (p * (dp - delta) * SCALE).astype(BF)
        acc[1, :, cols(h)] = jnp.dot(ds, q[:, cols(h)], preferred_element_type=F32)
        g = jnp.dot(kp[:, cols(h)].T, ds, preferred_element_type=F32)
        gq[:, cols(h)] = g.T.astype(BF)

    sent = []
    pending = []

    def arrive(cp):
        pending[:] = [c for c in pending if c is not cp]
        cp.wait_recv()

    def remote(src, dst, w, slot, dev):
        cp = pltpu.make_async_remote_copy(
            src, dst, ssem.at[w, slot], rsem.at[w, slot], device_id=dev, device_id_type=MESH
        )
        cp.start()
        sent.append(cp)
        pending.append(cp)
        return cp

    def natural(w, t, h, i):
        if w == 0:
            j = (2 * h + i) * 2 + ((1 - yl) if t == 0 else yl)
        else:
            j = ((z + 2 - t + 2 * h) % 4) * 2 + i
        return pl.ds(pl.multiple_of(j * DH, DH), DH)

    def half(w, t, h):
        return jnp.concatenate([acc[w, natural(w, t, h, i), :] for i in (0, 1)], axis=0)

    def at(start, size):
        return pl.ds(pl.multiple_of(start, size), size)

    pick = (par, yl)
    pick_dev = (other_par, other_yl)

    def swap_cores(w, t):
        xs[w, t] = half(w, t, 1 - core).astype(BF)
        return [remote(xs.at[w, t], xr.at[w, t], w, 16 * t + CORE, other_core)]

    def scatter(w, t, before):
        arrive(before[0])
        total = half(w, t, core) + xr[w, t].astype(F32)
        hs[w, t] = total
        rs[w, t] = total.astype(BF)
        out = []
        for d in (1, 2, 3):
            px, dev = x_dev(d)
            src = rs.at[w, t, at(px * BLK, BLK), :]
            out.append(remote(src, rr.at[w, t, d - 1], w, 16 * t + RS + d - 1, dev))
        return out

    def exchange(w, t, before):
        total = hs[w, t, at(x * BLK, BLK), :]
        for cp in before:
            arrive(cp)
        for d in range(3):
            total = total + rr[w, t, d].astype(F32)
        part[w, t] = total
        yb[w, t] = total.astype(BF)
        return [remote(yb.at[w, t], yx.at[w, t], w, 16 * t + YX, other_yh)]

    def gather(w, t, before):
        arrive(before[0])
        rows = at(core * QUART + x * BLK, BLK)
        agp[w, t, rows, :] = (part[w, t] + yx[w, t].astype(F32)).astype(BF)
        block = agp.at[w, t, rows, :]
        return [remote(block, block, w, 16 * t + AG + d - 1, x_dev(d)[1]) for d in (1, 2, 3)]

    def forward(w, t, before):
        for cp in before:
            arrive(cp)
        src = agp.at[w, t, at((2 * core + 1 - pick[w]) * DH, DH), :]
        dst = pag.at[w, t, at(core * DH, DH), :]
        sel = remote(src, dst, w, 16 * t + SEL, pick_dev[w])
        block = agp.at[w, t, at(core * QUART, QUART), :]
        return [remote(block, block, w, 16 * t + FWD, other_core), sel]

    def forward_picked(w, t, before):
        arrive(before[1])
        block = pag.at[w, t, at(core * DH, DH), :]
        return [before[0], remote(block, block, w, 16 * t + SEL2, other_core)]

    def own_product(w, t, full, before):
        arrive(before[0])
        rows = jnp.concatenate(
            [agp[w, t, at((2 * h + pick[w]) * DH, DH), :] for h in (0, 1)], axis=0
        )
        probs[2 * w + t, :, :QUART] = lax.dot_general(
            full[...], rows, NT, preferred_element_type=F32
        )
        for h in range(2):
            for i in range(2):
                b = 2 * h + i
                ag[w, natural(w, t, h, i), :] = agp[w, t, b * DH : (b + 1) * DH, :]

    def product(w, t, full2, before, relay=()):
        arrive(before[1])
        for cp in early[w]:
            if t == 0:
                arrive(cp)
        prod = probs[2 * w + t, :, :QUART] + lax.dot_general(
            full2[...], pag[w, t], NT, preferred_element_type=F32
        )
        blocks = [prod[:, h * DH : (h + 1) * DH] for h in range(2)]
        for cp in relay:
            arrive(cp)
        if relay:
            blocks[0] = jnp.concatenate(
                [blocks[0][:HALF] + zr[0].astype(F32), blocks[0][HALF:]], axis=0
            )
            blocks[1] = jnp.concatenate(
                [blocks[1][:HALF], blocks[1][HALF:] + zr[1].astype(F32)], axis=0
            )
        for h in range(2):
            pb[w, t, h] = blocks[h].astype(BF)

    def factor_v(t, before):
        product(0, t, vf2, before)
        return remote(pb.at[0, t, 1 - zi], zv.at[t], 0, Z1 + t, other_zi)

    def factor_k(before):
        product(1, 0, kf2, before)
        return [
            remote(pb.at[1, 0, 0, i * HALF : (i + 1) * HALF, :], zr.at[i], 1, Z1 + i, z_dev(d)[1])
            for i, d in ((0, 1), (1, 3))
        ]

    def relay_k(before, relay):
        product(1, 1, kf2, before, relay)
        return [
            remote(pb.at[1, 1, i], zk.at[i], 1, Z1 + 2 + i, z_dev(d)[1])
            for i, d in ((0, 1), (1, 3))
        ]

    def total_v(t, cp):
        arrive(cp)
        return pb[0, t, zi].astype(F32) + zv[t].astype(F32)

    def second_v(cp):
        ys[...] = total_v(0, cp).astype(BF)
        return remote(ys, yr, 0, Y1, other_yl)

    def finish_v(cp, y1):
        total = total_v(1, cp)
        arrive(y1)
        gvf[...] = (total + yr[...].astype(F32)).astype(BF)

    def finish_k(cps):
        t = pb[1, 0, 1].astype(F32)
        for i in range(2):
            arrive(cps[i])
            t = t + zk[i].astype(F32)
        gkf[...] = t.astype(BF)

    early = ([], [])

    def early_v():
        early[0].append(remote(vf_h, vf2, 0, FULL, other_par))

    def early_k(*pieces):
        for i in pieces:
            rows = slice(i * DH, (i + 1) * DH)
            early[1].append(remote(kf_h.at[rows, :], kf2.at[rows, :], 1, FULL + i, other_yl))

    def back(w, fac, out):
        out[...] = jnp.dot(fac[...], ag[w], preferred_element_type=F32).astype(BF)

    stage_a(0)
    for name in ("vp", "vf", "ff", "kf", "ef"):
        loads[name].start()
    stage_a(1)
    pl.semaphore_wait(bar, len(peers))
    early_v()
    early_k(0, 1, 2, 3)
    stage_a(2)
    stage_a(3)
    v0 = swap_cores(0, 0)
    v1 = swap_cores(0, 1)
    loads["vp"].wait()
    stage_b(0)
    v0 = scatter(0, 0, v0)
    v1 = scatter(0, 1, v1)
    stage_b(1)
    stage_b(2)
    v0 = exchange(0, 0, v0)
    stage_b(3)
    k0 = swap_cores(1, 0)
    k1 = swap_cores(1, 1)
    v1 = exchange(0, 1, v1)
    early_k(4, 5, 6, 7)
    v0 = gather(0, 0, v0)
    k0 = scatter(1, 0, k0)
    v1 = gather(0, 1, v1)
    k1 = scatter(1, 1, k1)
    v0 = forward(0, 0, v0)
    k0 = exchange(1, 0, k0)
    v1 = forward(0, 1, v1)
    v0 = forward_picked(0, 0, v0)
    k1 = exchange(1, 1, k1)
    k0 = gather(1, 0, k0)
    loads["vf"].wait()
    own_product(0, 0, vf, v0)
    zv0 = factor_v(0, v0)
    v1 = forward_picked(0, 1, v1)
    own_product(0, 1, vf, v1)
    zv1 = factor_v(1, v1)
    k1 = gather(1, 1, k1)
    k0 = forward(1, 0, k0)
    k1 = forward(1, 1, k1)
    k0 = forward_picked(1, 0, k0)
    loads["kf"].wait()
    own_product(1, 0, kf, k0)
    kz = factor_k(k0)
    k1 = forward_picked(1, 1, k1)
    own_product(1, 1, kf, k1)
    y1 = second_v(zv0)
    loads["ff"].wait()
    back(0, ff, gv)
    kz = relay_k(k1, kz)
    finish_v(zv1, y1)
    loads["ef"].wait()
    back(1, ef, gk)
    finish_k(kz)
    for cp in sent:
        cp.wait_send()


def hand_on(*refs):
    srcs, dsts, sem = refs[:5], refs[5:10], refs[10]
    copies = [pltpu.make_async_copy(s, d, sem.at[i]) for i, (s, d) in enumerate(zip(srcs, dsts))]
    for cp in copies:
        cp.start()
    for cp in copies:
        cp.wait()


def per_device(q, kf, vf, kp, vp, ef, ff, do):
    full = jax.ShapeDtypeStruct((TOK, COLS), BF)
    fac = jax.ShapeDtypeStruct((TOK, DH), BF)
    hbm = pl.BlockSpec(memory_space=pl.ANY)
    vm = pltpu.VMEM
    big = vm((TOK, COLS), BF)
    square = vm((TOK, ROWS), BF)
    made = pl.pallas_call(
        kernel,
        name="fused_backward",
        out_shape=(
            vm((TOK, COLS), BF), vm((TOK, COLS), BF), vm((TOK, COLS), BF),
            vm((TOK, DH), BF), vm((TOK, DH), BF),
        ),
        in_specs=[hbm] * 8,
        out_specs=[pl.BlockSpec(memory_space=vm)] * 5,
        scratch_shapes=[
            big, big, big, big, big, square, square, big,
            vm((4, ROWS, TOK), F32),
            vm((2, ROWS, COLS), F32),
            vm((2, 2, QUART, COLS), BF),
            vm((2, 2, QUART, COLS), BF),
            vm((2, 2, QUART, COLS), F32),
            vm((2, 2, QUART, COLS), BF),
            vm((2, 2, 3, BLK, COLS), BF),
            vm((2, 2, BLK, COLS), F32),
            vm((2, 2, BLK, COLS), BF),
            vm((2, 2, BLK, COLS), BF),
            vm((2, 2, HALF, COLS), BF),
            vm((2, ROWS, COLS), BF),
            big, big,
            vm((2, 2, QUART, COLS), BF),
            vm((2, 2, 2, TOK, DH), BF),
            vm((2, TOK, DH), BF),
            vm((2, HALF, DH), BF),
            vm((2, TOK, DH), BF),
            vm((TOK, DH), BF),
            vm((TOK, DH), BF),
            pltpu.SemaphoreType.DMA((17,)),
            pltpu.SemaphoreType.DMA((2, NSEM)),
            pltpu.SemaphoreType.DMA((2, NSEM)),
        ],
        compiler_params=pltpu.CompilerParams(
            collective_id=0, has_side_effects=True, vmem_limit_bytes=57 << 20
        ),
    )(q, kf, vf, kp, vp, ef, ff, do)
    return pl.pallas_call(
        hand_on,
        name="hand_on",
        out_shape=(full, full, full, fac, fac),
        in_specs=[pl.BlockSpec(memory_space=vm)] * 5,
        out_specs=[hbm] * 5,
        scratch_shapes=[pltpu.SemaphoreType.DMA((5,))],
        compiler_params=pltpu.CompilerParams(vmem_limit_bytes=1 << 20),
    )(*made)


def solution(mesh):
    whole = P("ctx", "head")
    placed = (
        whole, whole, whole, P(None, "head"), P(None, "head"),
        P("ctx", None), P("ctx", None), whole,
    )
    return jax.shard_map(
        per_device, mesh=mesh, in_specs=placed, out_specs=(whole,) * 5, check_vma=False
    )
```

```python
import functools

import jax
import jax.numpy as jnp
from jax import lax
from jax.experimental import pallas as pl
from jax.experimental.pallas import tpu as pltpu
from jax.sharding import PartitionSpec as P

DH = 128
SCALE = DH ** (-0.5)
SCALE_LOG2 = SCALE * 1.4426950408889634
BF = jnp.bfloat16
F32 = jnp.float32
MESH = pl.DeviceIdType.MESH
NT = (((1,), (1,)), ((), ()))

TOK = 1024
ROWS = 1024
COLS = 512
HALF = ROWS // 2
BLK = ROWS // 16
QUART = ROWS // 4

CORE, RS, YX, AG, FWD, SEL, SEL2, Z1, Y1, FULL, NSEM = 0, 1, 4, 5, 8, 9, 10, 32, 38, 39, 47


def kernel(
    q_h, kf_h, vf_h, kp_h, vp_h, e_h, f_h, do_h,
    gq, gk, gv, gkf, gvf,
    q, kf, vf, kp, vp, ef, ff, do,
    probs, acc, xs, xr, hs, rs, rr, part, yb, yx, agp, ag, vf2, kf2, pag, pb, zv, zr, zk, ys, yr,
    in_sem, ssem, rsem,
):
    ctx = lax.axis_index("ctx")
    head = lax.axis_index("head")
    yh, x, core = ctx // 8, (ctx // 2) % 4, ctx % 2
    z, yl = head // 2, head % 2

    def x_dev(d):
        px = (x + d) % 4
        return px, (yh * 8 + px * 2 + core, head)

    def z_dev(d):
        pz = (z + d) % 4
        return pz, (ctx, pz * 2 + yl)

    par, zi = z % 2, z // 2
    other_par = (ctx, (zi * 2 + (1 - par)) * 2 + yl)
    other_zi = (ctx, ((1 - zi) * 2 + par) * 2 + yl)
    other_yh = ((1 - yh) * 8 + x * 2 + core, head)
    other_core = (yh * 8 + x * 2 + (1 - core), head)
    other_yl = (ctx, z * 2 + (1 - yl))

    def cols(h):
        return slice(h * DH, (h + 1) * DH)

    head_loads = [
        [
            pltpu.make_async_copy(src.at[:, cols(h)], dst.at[:, cols(h)], in_sem.at[5 + 3 * h + i])
            for i, (src, dst) in enumerate(((q_h, q), (kp_h, kp), (do_h, do)))
        ]
        for h in range(4)
    ]
    for cps in head_loads:
        for cp in cps:
            cp.start()
    loads = {
        name: pltpu.make_async_copy(src, dst, in_sem.at[i])
        for i, (name, src, dst) in enumerate((
            ("vp", vp_h, vp), ("vf", vf_h, vf), ("ff", f_h, ff), ("kf", kf_h, kf), ("ef", e_h, ef),
        ))
    }

    bar = pltpu.get_barrier_semaphore()
    peers = [other_core, other_yl, other_yh]
    peers += [x_dev(d)[1] for d in (1, 2, 3)] + [z_dev(d)[1] for d in (1, 2, 3)]
    for p in peers:
        pl.semaphore_signal(bar, inc=1, device_id=p, device_id_type=MESH)

    def stage_a(h):
        for cp in head_loads[h]:
            cp.wait()
        s = lax.dot_general(kp[:, cols(h)], q[:, cols(h)], NT, preferred_element_type=F32)
        m = jnp.max(s, axis=0, keepdims=True)
        e = jnp.exp2((s - m) * SCALE_LOG2)
        l = jnp.sum(e, axis=0, keepdims=True)
        p = e * (1.0 / l)
        probs[h] = p
        acc[0, :, cols(h)] = jnp.dot(p.astype(BF), do[:, cols(h)], preferred_element_type=F32)

    def stage_b(h):
        dp = lax.dot_general(vp[:, cols(h)], do[:, cols(h)], NT, preferred_element_type=F32)
        p = probs[h]
        delta = jnp.sum(p.astype(BF).astype(F32) * dp, axis=0, keepdims=True)
        ds = (p * (dp - delta) * SCALE).astype(BF)
        acc[1, :, cols(h)] = jnp.dot(ds, q[:, cols(h)], preferred_element_type=F32)
        g = jnp.dot(kp[:, cols(h)].T, ds, preferred_element_type=F32)
        gq[:, cols(h)] = g.T.astype(BF)

    sent = []
    pending = []

    def arrive(cp):
        pending[:] = [c for c in pending if c is not cp]
        cp.wait_recv()

    def remote(src, dst, w, slot, dev):
        cp = pltpu.make_async_remote_copy(
            src, dst, ssem.at[w, slot], rsem.at[w, slot], device_id=dev, device_id_type=MESH
        )
        cp.start()
        sent.append(cp)
        pending.append(cp)
        return cp

    def natural(w, t, h, i):
        if w == 0:
            j = (2 * h + i) * 2 + ((1 - yl) if t == 0 else yl)
        else:
            j = ((z + 2 - t + 2 * h) % 4) * 2 + i
        return pl.ds(pl.multiple_of(j * DH, DH), DH)

    def half(w, t, h):
        return jnp.concatenate([acc[w, natural(w, t, h, i), :] for i in (0, 1)], axis=0)

    def at(start, size):
        return pl.ds(pl.multiple_of(start, size), size)

    pick = (par, yl)
    pick_dev = (other_par, other_yl)

    def swap_cores(w, t):
        xs[w, t] = half(w, t, 1 - core).astype(BF)
        return [remote(xs.at[w, t], xr.at[w, t], w, 16 * t + CORE, other_core)]

    def scatter(w, t, before):
        arrive(before[0])
        total = half(w, t, core) + xr[w, t].astype(F32)
        hs[w, t] = total
        rs[w, t] = total.astype(BF)
        out = []
        for d in (2, 1, 3):
            px, dev = x_dev(d)
            src = rs.at[w, t, at(px * BLK, BLK), :]
            out.append(remote(src, rr.at[w, t, d - 1], w, 16 * t + RS + d - 1, dev))
        return out

    def exchange(w, t, before):
        total = hs[w, t, at(x * BLK, BLK), :]
        for cp in before:
            arrive(cp)
        for d in range(3):
            total = total + rr[w, t, d].astype(F32)
        part[w, t] = total
        yb[w, t] = total.astype(BF)
        return [remote(yb.at[w, t], yx.at[w, t], w, 16 * t + YX, other_yh)]

    def gather(w, t, before):
        arrive(before[0])
        rows = at(core * QUART + x * BLK, BLK)
        agp[w, t, rows, :] = (part[w, t] + yx[w, t].astype(F32)).astype(BF)
        block = agp.at[w, t, rows, :]
        return [remote(block, block, w, 16 * t + AG + d - 1, x_dev(d)[1]) for d in (2, 1, 3)]

    def forward(w, t, before):
        for cp in before:
            arrive(cp)
        src = agp.at[w, t, at((2 * core + 1 - pick[w]) * DH, DH), :]
        dst = pag.at[w, t, at(core * DH, DH), :]
        sel = remote(src, dst, w, 16 * t + SEL, pick_dev[w])
        block = agp.at[w, t, at(core * QUART, QUART), :]
        return [remote(block, block, w, 16 * t + FWD, other_core), sel]

    def forward_picked(w, t, before):
        arrive(before[1])
        block = pag.at[w, t, at(core * DH, DH), :]
        return [before[0], remote(block, block, w, 16 * t + SEL2, other_core)]

    def own_product(w, t, full, before):
        arrive(before[0])
        rows = jnp.concatenate(
            [agp[w, t, at((2 * h + pick[w]) * DH, DH), :] for h in (0, 1)], axis=0
        )
        probs[2 * w + t, :, :QUART] = lax.dot_general(
            full[...], rows, NT, preferred_element_type=F32
        )

    def product(w, t, full2, before):
        arrive(before[1])
        for cp in early[w]:
            if t == 0:
                arrive(cp)
        prod = probs[2 * w + t, :, :QUART] + lax.dot_general(
            full2[...], pag[w, t], NT, preferred_element_type=F32
        )
        blocks = [prod[:, h * DH : (h + 1) * DH] for h in range(2)]
        if w == 1 and t == 1:
            return blocks
        for h in range(2):
            pb[w, t, h] = blocks[h].astype(BF)

    def factor_v(t, before):
        product(0, t, vf2, before)
        return remote(pb.at[0, t, 1 - zi], zv.at[t], 0, Z1 + t, other_zi)

    def factor_k(before):
        product(1, 0, kf2, before)
        return [
            remote(pb.at[1, 0, 0, i * HALF : (i + 1) * HALF, :], zr.at[i], 1, Z1 + i, z_dev(d)[1])
            for i, d in ((0, 1), (1, 3))
        ]

    def relay_k(before, relay):
        blocks = product(1, 1, kf2, before)
        halves = (slice(0, HALF), slice(HALF, TOK))
        out = []

        def send(i, rows, slot):
            src, dst = pb.at[1, 1, i, rows, :], zk.at[i, rows, :]
            out.append(remote(src, dst, 1, Z1 + slot, z_dev(1 + 2 * i)[1]))

        for i in range(2):
            rows = halves[1 - i]
            pb[1, 1, i, rows, :] = blocks[i][rows].astype(BF)
            send(i, rows, 2 + i)
        for i in range(2):
            rows = halves[i]
            arrive(relay[i])
            pb[1, 1, i, rows, :] = (blocks[i][rows] + zr[i].astype(F32)).astype(BF)
            send(i, rows, 4 + i)
        return out

    def total_v(t, cp):
        arrive(cp)
        return pb[0, t, zi].astype(F32) + zv[t].astype(F32)

    def second_v(cp):
        ys[...] = total_v(0, cp).astype(BF)
        return remote(ys, yr, 0, Y1, other_yl)

    def finish_v(cp, y1):
        total = total_v(1, cp)
        arrive(y1)
        gvf[...] = (total + yr[...].astype(F32)).astype(BF)

    def finish_k(cps):
        t = pb[1, 0, 1].astype(F32)
        for cp in cps:
            arrive(cp)
        for i in range(2):
            t = t + zk[i].astype(F32)
        gkf[...] = t.astype(BF)

    early = ([], [])

    def early_v():
        early[0].append(remote(vf_h, vf2, 0, FULL, other_par))

    def early_k(*pieces):
        for i in pieces:
            rows = slice(i * DH, (i + 1) * DH)
            early[1].append(remote(kf_h.at[rows, :], kf2.at[rows, :], 1, FULL + i, other_yl))

    def back(w, fac, out):
        for t in range(2):
            for b in range(4):
                rows = natural(w, t, b // 2, b % 2)
                ag[w, rows, :] = agp[w, t, b * DH : (b + 1) * DH, :]
        out[...] = jnp.dot(fac[...], ag[w], preferred_element_type=F32).astype(BF)

    stage_a(0)
    for name in ("vp", "vf", "ff", "kf", "ef"):
        loads[name].start()
    stage_a(1)
    pl.semaphore_wait(bar, len(peers))
    early_v()
    early_k(0, 1, 2, 3)
    stage_a(2)
    stage_a(3)
    v0 = swap_cores(0, 0)
    v1 = swap_cores(0, 1)
    loads["vp"].wait()
    stage_b(0)
    v0 = scatter(0, 0, v0)
    v1 = scatter(0, 1, v1)
    stage_b(1)
    stage_b(2)
    v0 = exchange(0, 0, v0)
    stage_b(3)
    k0 = swap_cores(1, 0)
    k1 = swap_cores(1, 1)
    v1 = exchange(0, 1, v1)
    early_k(4, 5, 6, 7)
    v0 = gather(0, 0, v0)
    k0 = scatter(1, 0, k0)
    v1 = gather(0, 1, v1)
    k1 = scatter(1, 1, k1)
    v0 = forward(0, 0, v0)
    k0 = exchange(1, 0, k0)
    v1 = forward(0, 1, v1)
    v0 = forward_picked(0, 0, v0)
    loads["vf"].wait()
    own_product(0, 0, vf, v0)
    k0 = gather(1, 0, k0)
    k1 = exchange(1, 1, k1)
    zv0 = factor_v(0, v0)
    v1 = forward_picked(0, 1, v1)
    own_product(0, 1, vf, v1)
    zv1 = factor_v(1, v1)
    k1 = gather(1, 1, k1)
    k0 = forward(1, 0, k0)
    k1 = forward(1, 1, k1)
    k0 = forward_picked(1, 0, k0)
    loads["kf"].wait()
    own_product(1, 0, kf, k0)
    kz = factor_k(k0)
    y1 = second_v(zv0)
    k1 = forward_picked(1, 1, k1)
    own_product(1, 1, kf, k1)
    loads["ff"].wait()
    back(0, ff, gv)
    kz = relay_k(k1, kz)
    finish_v(zv1, y1)
    loads["ef"].wait()
    back(1, ef, gk)
    finish_k(kz)
    for cp in sent:
        cp.wait_send()


def hand_on(*refs):
    srcs, dsts, sem = refs[:5], refs[5:10], refs[10]
    copies = [pltpu.make_async_copy(s, d, sem.at[i]) for i, (s, d) in enumerate(zip(srcs, dsts))]
    for cp in copies:
        cp.start()
    for cp in copies:
        cp.wait()


def per_device(q, kf, vf, kp, vp, ef, ff, do):
    full = jax.ShapeDtypeStruct((TOK, COLS), BF)
    fac = jax.ShapeDtypeStruct((TOK, DH), BF)
    hbm = pl.BlockSpec(memory_space=pl.ANY)
    vm = pltpu.VMEM
    big = vm((TOK, COLS), BF)
    square = vm((TOK, ROWS), BF)
    made = pl.pallas_call(
        kernel,
        name="fused_backward",
        out_shape=(
            vm((TOK, COLS), BF), vm((TOK, COLS), BF), vm((TOK, COLS), BF),
            vm((TOK, DH), BF), vm((TOK, DH), BF),
        ),
        in_specs=[hbm] * 8,
        out_specs=[pl.BlockSpec(memory_space=vm)] * 5,
        scratch_shapes=[
            big, big, big, big, big, square, square, big,
            vm((4, ROWS, TOK), F32),
            vm((2, ROWS, COLS), F32),
            vm((2, 2, QUART, COLS), BF),
            vm((2, 2, QUART, COLS), BF),
            vm((2, 2, QUART, COLS), F32),
            vm((2, 2, QUART, COLS), BF),
            vm((2, 2, 3, BLK, COLS), BF),
            vm((2, 2, BLK, COLS), F32),
            vm((2, 2, BLK, COLS), BF),
            vm((2, 2, BLK, COLS), BF),
            vm((2, 2, HALF, COLS), BF),
            vm((2, ROWS, COLS), BF),
            big, big,
            vm((2, 2, QUART, COLS), BF),
            vm((2, 2, 2, TOK, DH), BF),
            vm((2, TOK, DH), BF),
            vm((2, HALF, DH), BF),
            vm((2, TOK, DH), BF),
            vm((TOK, DH), BF),
            vm((TOK, DH), BF),
            pltpu.SemaphoreType.DMA((17,)),
            pltpu.SemaphoreType.DMA((2, NSEM)),
            pltpu.SemaphoreType.DMA((2, NSEM)),
        ],
        compiler_params=pltpu.CompilerParams(
            collective_id=0, has_side_effects=True, vmem_limit_bytes=57 << 20
        ),
    )(q, kf, vf, kp, vp, ef, ff, do)
    return pl.pallas_call(
        hand_on,
        name="hand_on",
        out_shape=(full, full, full, fac, fac),
        in_specs=[pl.BlockSpec(memory_space=vm)] * 5,
        out_specs=[hbm] * 5,
        scratch_shapes=[pltpu.SemaphoreType.DMA((5,))],
        compiler_params=pltpu.CompilerParams(vmem_limit_bytes=1 << 20),
    )(*made)


def solution(mesh):
    whole = P("ctx", "head")
    placed = (
        whole, whole, whole, P(None, "head"), P(None, "head"),
        P("ctx", None), P("ctx", None), whole,
    )
    return jax.shard_map(
        per_device, mesh=mesh, in_specs=placed, out_specs=(whole,) * 5, check_vma=False
    )
```
